32 devices in a mesh: groups: 1, ep: 16 (over z, y, x), wr: 2 (over core).
Axes of the slice: x: 2, y: 2, z: 4, core: 2. Of those that a mesh axis runs over, the one named last changes fastest.
Arguments:
- hidden: bfloat16 [2048, 8, 1024], P(('groups', 'ep'), None, 'wr'), may hold values from -6 to 6
- weight: bfloat16 [16, 1024, 3584], P('ep', None, 'wr'), may hold values from -0.1875 to 0.1875
- expert_ids: int32 [2048, 8], P(('groups', 'ep')), may hold values from 0 to 15, all different within a row; in each aligned block of 64 rows (0 to 63, 64 to 127, ...) at most 40 rows name the same one
- gate_score: int32 [2048, 8], P(('groups', 'ep')), may hold values from 1 to 64
Outputs:
- mixed: bfloat16 [2048, 3584], P(('groups', 'ep'), 'wr')
The draws below stay inside these ranges and needn't reach their ends.
Inputs may be any that keep to these rules, and one draw needn't show every extreme that they name: `expert_ids`: each token names 8 different experts; in each aligned block of 64 tokens no expert is named by more than 40 tokens, and in every draw some block has an expert named by exactly 40 tokens.
All inputs are finite; a program needn't handle non-finite values.
Results may differ from the reference program's by a relative error of at most 0.0049.
Values may be sent and summed in bfloat16 or wider, within the bound.
A program may use at most 64 MiB of HBM per device.

```python
import math
import jax
import jax.numpy as jnp
import numpy as np
from jax import lax

D = 3584
H = 1024
TOP = 8
TOK_DEV = 128
EXPERTS = 16
TOKENS = 2048
CAP = 40


def with_ends(entries, own_key, low, largest):
    longest = entries.shape.index(max(entries.shape))
    spots = []
    for shift in (0, 1):
        where = [jax.random.randint(jax.random.fold_in(own_key, axis), (), 0, length) for axis, length in enumerate(entries.shape)]
        where[longest] = (where[longest] + shift) % entries.shape[longest]
        spots.append(tuple(where))
    return entries.at[spots[0]].set(low).at[spots[1]].set(largest)


def steps_of(own_key, extent, split, smallest, largest):
    loudness = 1.0
    for axis_at, parts in split:
        draws = jax.random.uniform(jax.random.fold_in(jax.random.fold_in(own_key, 6), axis_at), (parts,), jnp.float32, smallest / len(split), largest / len(split))
        loudness = loudness * jnp.repeat(jnp.exp(draws), extent[axis_at] // parts).reshape((-1,) + (1,) * (len(extent) - 1 - axis_at))
    return loudness


def shared_out(own_key, own, number, rows, count, top, limit, lean):
    sequence = jax.random.permutation(own_key, count)
    packed, ordinary = load_shares(count, rows * top, limit, lean, True), load_shares(count, rows * top, limit, lean, False)
    places = jnp.arange(count)

    def named(tallies, offset_by):
        used = int((tallies > 0).sum())
        fixed = max(1, used // 4)
        moved = fixed + (places - fixed + offset_by * (used - fixed)) % max(1, count - fixed)
        return jnp.zeros((count,), jnp.int32).at[sequence[jnp.where(places < fixed, places, moved)]].set(jnp.asarray(tallies, jnp.int32))

    tallies = jnp.where(number % 4 == 0, named(packed, number // 4), named(ordinary, number - number // 4 - 1))
    mixed = jax.random.permutation(jax.random.fold_in(own, 3), count)
    giver, receiver = mixed[0:count // 2 * 2:2], mixed[1:count // 2 * 2:2]
    margin = jnp.minimum(tallies[giver] - 1, limit - tallies[receiver]) // 2
    margin = jnp.where((giver == sequence[0]) | (receiver == sequence[0]) | (tallies[receiver] == 0), 0, jnp.maximum(margin, 0))
    moved = jax.random.randint(jax.random.fold_in(own, 4), (count // 2,), 0, 1 << 20) % (margin + 1)
    tallies = tallies.at[giver].add(-moved).at[receiver].add(moved)
    items = jnp.searchsorted(jnp.cumsum(tallies), jnp.arange(rows * top), side="right").astype(jnp.int32)
    grid = items.reshape(top, rows).T
    grid = grid[jax.random.permutation(jax.random.fold_in(own, 1), rows)]
    offset_by = jax.random.randint(jax.random.fold_in(own, 2), (rows, 1), 0, top)
    return jnp.take_along_axis(grid, (jnp.arange(top)[None, :] + offset_by) % top, axis=1)


def load_shares(number_of, total, most, skew, full):
    weights = [(1 << 20) // math.isqrt(standing ** skew) + 1 for standing in range(1, number_of + 1)]
    largest = most if full else min(most, max(-(-total // number_of), total * weights[0] // sum(weights)))
    least = 1 if total - largest >= number_of - 1 else 0
    holding, surplus = [largest] + [least] * (number_of - 1), total - largest - least * (number_of - 1)
    while surplus > 0:
        candidates = [i for i in range(1, number_of) if holding[i] < largest] or [i for i in range(1, number_of) if holding[i] < most]
        whole, budget = sum([weights[i] for i in candidates]), surplus
        for i in candidates:
            extra = min(most - holding[i], max(1, budget * weights[i] // whole), surplus)
            holding[i] = holding[i] + extra
            surplus = surplus - extra
    return np.array(holding)


def gaussian(stream_key, extent, spread, reach, pieces=(), kind=jnp.bfloat16):
    drawn = spread * jax.random.normal(stream_key, extent, jnp.float32)
    if pieces:
        drawn = drawn * steps_of(stream_key, extent, pieces, -0.22, 0.18)
    return jnp.clip(drawn, -reach, reach).astype(kind)


def setup_inputs(seed: int = 0, part: int = 0) -> dict:
    key_list = jax.random.split(jax.random.key(seed), 5)
    part_keys = jax.random.split(jax.random.fold_in(key_list[4], part), 5)
    hidden = gaussian(part_keys[0], (TOKENS, TOP, H), 1.0, 6.0, ((0, 16), (2, 2)))
    weight = gaussian(key_list[1], (EXPERTS, H, D), H ** -0.5, 0.1875, ((0, 16), (2, 2)))
    expert_ids_keys = jax.random.split(jax.random.fold_in(part_keys[2], 1), TOKENS // (TOK_DEV // 2))
    expert_ids_turns = jax.random.permutation(jax.random.fold_in(part_keys[2], 3), TOKENS // (TOK_DEV // 2))
    expert_ids = jax.vmap(lambda own, number: shared_out(jax.random.fold_in(part_keys[2], 2), own, number, TOK_DEV // 2, EXPERTS, TOP, CAP, 1))(expert_ids_keys, expert_ids_turns).reshape((TOKENS, TOP))
    gate_score = with_ends(jax.random.randint(part_keys[3], (TOKENS, TOP), 1, 65), jax.random.fold_in(part_keys[3], 1), 1, 64).astype(jnp.int32)
    return {"hidden": hidden, "weight": weight, "expert_ids": expert_ids, "gate_score": gate_score}


def mixing(gate_score):
    score = gate_score.astype(jnp.float32)
    return 2.827 * score / jnp.sum(score, axis=1, keepdims=True)


def slot_numbers(ids_flat, experts, block_pairs):
    onehot = (ids_flat[:, None] == jnp.arange(experts, dtype=jnp.int32)[None, :]).astype(jnp.int32)
    grouped = onehot.reshape(-1, block_pairs, experts)
    before = jnp.cumsum(grouped, axis=1) - grouped
    return jnp.sum(before * grouped, axis=2).reshape(-1).astype(jnp.int32)


def reference(hidden, weight, expert_ids, gate_score):
    gates = mixing(gate_score)
    pairs = TOKENS * TOP
    ids_flat = expert_ids.reshape(-1).astype(jnp.int32)
    block_pairs = (TOK_DEV // 2) * TOP
    slot = slot_numbers(ids_flat, EXPERTS, block_pairs)
    block = jnp.arange(pairs, dtype=jnp.int32) // block_pairs
    blocks = pairs // block_pairs
    table = jnp.full((EXPERTS, blocks * CAP), pairs, jnp.int32)
    table = table.at[ids_flat, block * CAP + slot].set(jnp.arange(pairs, dtype=jnp.int32))
    rows_pad = jnp.concatenate((hidden.reshape(pairs, H), jnp.zeros((1, H), jnp.bfloat16)), 0)
    gates_pad = jnp.concatenate((gates.reshape(-1), jnp.zeros((1,), jnp.float32)), 0)

    def one_expert(total, inputs):
        index, matrix = inputs
        output = jnp.dot(rows_pad[index], matrix, preferred_element_type=jnp.float32).astype(jnp.bfloat16)
        output = lax.optimization_barrier(output).astype(jnp.float32)
        total = total.at[index // TOP].add(output * gates_pad[index][:, None], mode="drop")
        return total, None

    total = lax.scan(one_expert, jnp.zeros((TOKENS, D), jnp.float32), (table, weight))[0]
    return total.astype(jnp.bfloat16)
```

```python
import functools

import jax
import jax.numpy as jnp
from jax import lax
from jax.experimental import pallas as pl
from jax.experimental.pallas import tpu as pltpu
from jax.sharding import PartitionSpec as P

MESH = pl.DeviceIdType.MESH
ORDER = (3, 1, 2, 0)
EMPTY = 255.0
TILE = 256


def partner(index, step):
    if step == 0:
        return index
    if step == 1:
        return index + 1 - 2 * (index % 2)
    if step == 2:
        return index + 2 - 4 * (index // 2)
    return 3 - index


def iota(shape, axis):
    return lax.broadcasted_iota(jnp.int32, shape, axis)


def onehot(condition):
    return condition.astype(jnp.float32).astype(jnp.bfloat16)


def mm(a, b):
    return jnp.dot(a, b, preferred_element_type=jnp.float32)


def kernel(rows, ids_ref, score_ref, flat_ref, hidden_ref, weight_hbm, out_ref,
           weight, outgoing, arrived, result, planar, table, zsend, zrecv,
           wsem, d_send, d_recv, f_send, f_recv, p_send, p_recv,
           t_send, t_recv, z_send, z_recv):
    me, w = lax.axis_index("ep"), lax.axis_index("wr")
    zm, pm = me // 4, me % 4
    tokens, top = ids_ref.shape
    pairs, part = hidden_ref.shape
    group = 4 * rows
    width = out_ref.shape[1]

    load = pltpu.make_async_copy(weight_hbm, weight, wsem)
    load.start()

    barrier = pltpu.get_barrier_semaphore()
    for j in range(4):
        for q in range(4):
            if j or q:
                pl.semaphore_signal(
                    barrier, inc=1, device_id_type=MESH,
                    device_id={"ep": partner(zm, j) * 4 + partner(pm, q), "wr": w})
    pl.semaphore_signal(barrier, inc=1, device_id_type=MESH, device_id={"ep": me, "wr": 1 - w})

    flat = flat_ref[...]
    named = onehot(flat == iota((16, pairs), 0))
    earlier = onehot(iota((pairs, pairs), 0) < iota((pairs, pairs), 1))
    slot = jnp.sum(mm(named, earlier) * named.astype(jnp.float32), axis=0, keepdims=True)
    target = flat * rows + slot.astype(jnp.int32)

    def block(ref, j, p):
        return ref.at[j, pl.ds(pl.multiple_of(p * rows, 16), rows)]

    pl.semaphore_wait(barrier, 16)

    dispatch = {}
    for j in ORDER:
        zd = partner(zm, j)
        pick = onehot(target - zd * group == iota((group, pairs), 0))
        outgoing[j] = mm(pick, hidden_ref[...]).astype(jnp.bfloat16)
        for q in range(4):
            pd = partner(pm, q)
            if j == 0 and q == 0:
                arrived[w, 0, pl.ds(pl.multiple_of(pm * rows, 16), rows)] = (
                    outgoing[0, pl.ds(pl.multiple_of(pm * rows, 16), rows)])
                continue
            copy = pltpu.make_async_remote_copy(
                src_ref=block(outgoing, j, pd),
                dst_ref=arrived.at[w, j, pl.ds(pl.multiple_of(pm * rows, 16), rows)],
                send_sem=d_send.at[j, q], recv_sem=d_recv.at[j, q],
                device_id={"ep": zd * 4 + pd, "wr": w}, device_id_type=MESH)
            copy.start()
            dispatch[j, q] = copy

    ids, score = ids_ref[...], score_ref[...]
    lane = iota((tokens, 16), 1)
    scores = jnp.zeros((tokens, 16), jnp.float32)
    for k in range(top):
        scores = scores + jnp.where(
            ids[:, k:k + 1] == lane, score[:, k:k + 1].astype(jnp.float32), 0.0)
    gates = 2.827 * scores / jnp.sum(scores, axis=1, keepdims=True)
    before = mm(onehot(iota((tokens, tokens), 1) < iota((tokens, tokens), 0)), onehot(scores > 0))
    place = jnp.where(scores > 0, before, EMPTY).astype(jnp.bfloat16)
    high = gates.astype(jnp.bfloat16)
    low = (gates - high.astype(jnp.float32)).astype(jnp.bfloat16)

    def put(values, shift):
        return mm(values, onehot(iota((16, 128), 0) + shift == iota((16, 128), 1)))

    table[0] = (put(place, 0) + put(high, 16) + put(low, 32)).astype(jnp.bfloat16)
    tables = {}
    for j in range(1, 4):
        tables[j] = pltpu.make_async_remote_copy(
            src_ref=table.at[0], dst_ref=table.at[j],
            send_sem=t_send.at[j], recv_sem=t_recv.at[j],
            device_id={"ep": partner(zm, j) * 4 + pm, "wr": w}, device_id_type=MESH)
        tables[j].start()

    planars, forwards, zcopies = {}, {}, {}

    def forward(j):
        for q in range(4):
            if j or q:
                dispatch[j, q].wait_recv()
        forwards[j] = pltpu.make_async_remote_copy(
            src_ref=arrived.at[w, j], dst_ref=arrived.at[w, j],
            send_sem=f_send.at[j], recv_sem=f_recv.at[j],
            device_id={"ep": me, "wr": 1 - w}, device_id_type=MESH)
        forwards[j].start()

    def expert(j):
        forwards[j].wait_recv()

        @pl.loop(0, width // TILE)
        def _(i):
            cols = pl.ds(pl.multiple_of(i * TILE, TILE), TILE)
            total = mm(arrived[0, j], weight[:part, cols]) + mm(arrived[1, j], weight[part:, cols])
            result[j, :, cols] = total.astype(jnp.bfloat16)

        for q in range(1, 4):
            pd = partner(pm, q)
            planars[j, q] = pltpu.make_async_remote_copy(
                src_ref=block(result, j, pd), dst_ref=block(planar, j, pm),
                send_sem=p_send.at[j, q], recv_sem=p_recv.at[j, q],
                device_id={"ep": zm * 4 + pd, "wr": w}, device_id_type=MESH)
            planars[j, q].start()
        own = pl.ds(pl.multiple_of(pm * rows, 16), rows)
        planar[j, own] = result[j, own]

    def combine(j):
        if j:
            tables[j].wait_recv()
        info = table[j]
        column = iota((128, group), 1)
        quarter = sum((column >= n * rows).astype(jnp.int32) for n in range(1, 4))
        source = zm * 4 + quarter

        def spread(shift):
            return mm(info, onehot(iota((128, group), 0) == source + shift))

        wide = iota((tokens, group), 1)
        within = wide - rows * sum((wide >= n * rows).astype(jnp.int32) for n in range(1, 4))
        hit = spread(0) == within.astype(jnp.float32)
        high = jnp.where(hit, spread(16), 0.0).astype(jnp.bfloat16)
        low = jnp.where(hit, spread(32), 0.0).astype(jnp.bfloat16)
        for q in range(1, 4):
            planars[j, q].wait_recv()
        if j == 2:
            zcopies[3].wait_recv()
        if j == 0:
            zcopies[1].wait_recv()
            zcopies[2].wait_recv()

        @pl.loop(0, width // TILE)
        def _(i):
            cols = pl.ds(pl.multiple_of(i * TILE, TILE), TILE)
            values = planar[j, :, cols]
            total = mm(high, values) + mm(low, values)
            if j == 2:
                total = total + zrecv[3, :, cols].astype(jnp.float32)
            if j == 0:
                total = (total + zrecv[1, :, cols].astype(jnp.float32)
                         + zrecv[2, :, cols].astype(jnp.float32))
                out_ref[:, cols] = total.astype(jnp.bfloat16)
            else:
                zsend[j, :, cols] = total.astype(jnp.bfloat16)

        if j:
            zcopies[j] = pltpu.make_async_remote_copy(
                src_ref=zsend.at[j], dst_ref=zrecv.at[j],
                send_sem=z_send.at[j], recv_sem=z_recv.at[j],
                device_id={"ep": partner(zm, 2 if j == 2 else 1) * 4 + pm, "wr": w},
                device_id_type=MESH)
            zcopies[j].start()

    load.wait()
    for n, j in enumerate(ORDER):
        forward(j)
        expert(j)
        if n:
            combine(ORDER[n - 1])
    combine(ORDER[-1])

    for copies in (dispatch, tables, forwards, planars, zcopies):
        for copy in copies.values():
            copy.wait_send()


def by_kernel(hidden, weight, expert_ids, gate_score):
    tokens, top, part = hidden.shape
    full, width = weight.shape[1:]
    pairs = tokens * top
    rows = 2 * (5 * pairs // 2 // (4 * 16))
    group = 4 * rows
    bf16 = jnp.bfloat16
    vmem = pl.BlockSpec(memory_space=pltpu.VMEM)
    dma = pltpu.SemaphoreType.DMA
    return pl.pallas_call(
        functools.partial(kernel, rows),
        out_shape=jax.ShapeDtypeStruct((tokens, width), bf16),
        in_specs=[vmem, vmem, vmem, vmem, pl.BlockSpec(memory_space=pl.ANY)],
        out_specs=vmem,
        scratch_shapes=[
            pltpu.VMEM((full, width), bf16),
            pltpu.VMEM((4, group, part), bf16),
            pltpu.VMEM((2, 4, group, part), bf16),
            pltpu.VMEM((4, group, width), bf16),
            pltpu.VMEM((4, group, width), bf16),
            pltpu.VMEM((4, tokens, 128), bf16),
            pltpu.VMEM((4, tokens, width), bf16),
            pltpu.VMEM((4, tokens, width), bf16),
            dma, dma((4, 4)), dma((4, 4)), dma((4,)), dma((4,)), dma((4, 4)), dma((4, 4)),
            dma((4,)), dma((4,)), dma((4,)), dma((4,)),
        ],
        compiler_params=pltpu.CompilerParams(
            collective_id=0, has_side_effects=True, vmem_limit_bytes=50 * 1024 * 1024),
        cost_estimate=pl.CostEstimate(
            flops=2 * 16 * rows * full * width, bytes_accessed=2 * full * width, transcendentals=0),
    )(expert_ids, gate_score, expert_ids.reshape(1, pairs), hidden.reshape(pairs, part), weight[0])


def mixing(gate_score):
    score = gate_score.astype(jnp.float32)
    return 2.827 * score / jnp.sum(score, axis=1, keepdims=True)


def slot_numbers(ids_flat, experts, block_pairs):
    onehot = (ids_flat[:, None] == jnp.arange(experts, dtype=jnp.int32)[None, :]).astype(jnp.int32)
    grouped = onehot.reshape(-1, block_pairs, experts)
    before = jnp.cumsum(grouped, axis=1) - grouped
    return jnp.sum(before * grouped, axis=2).reshape(-1)


def by_collectives(hidden, weight, expert_ids, gate_score):
    tok_dev, top, part_width = hidden.shape
    experts = lax.axis_size("ep")
    half = tok_dev // 2
    cap = max(2, 5 * half * top // (4 * experts))
    side = lax.axis_index("wr")
    gates = mixing(gate_score)
    local_weight = weight[0]
    source = lax.all_gather(hidden, "wr", axis=2, tiled=True)
    start = side * half
    mine = lax.dynamic_slice_in_dim(source, start, half, 0)
    my_ids = lax.dynamic_slice_in_dim(expert_ids, start, half, 0).reshape(-1)
    my_gates = lax.dynamic_slice_in_dim(gates, start, half, 0)
    slot = slot_numbers(my_ids, experts, half * top)
    target = my_ids * cap + slot
    row_width = mine.shape[2]
    outgoing = (
        jnp.zeros((experts * cap, row_width), jnp.bfloat16)
        .at[target]
        .set(mine.reshape(half * top, row_width))
    )
    outgoing = outgoing.reshape(experts, cap, row_width)
    received = lax.all_to_all(outgoing, "ep", split_axis=0, concat_axis=0, tiled=True)
    result = jnp.einsum(
        "scj,jd->scd",
        received,
        lax.all_gather(local_weight, "wr", axis=1, tiled=True),
        preferred_element_type=jnp.float32,
    ).astype(jnp.bfloat16)
    returned = lax.all_to_all(result, "ep", split_axis=0, concat_axis=0, tiled=True)
    full_width = returned.shape[2]
    picked = returned.reshape(experts * cap, full_width)[target]
    weighted = picked.astype(jnp.float32).reshape(half, top, full_width) * my_gates[:, :, None]
    partial_out = jnp.sum(weighted, axis=1).astype(jnp.bfloat16)
    return lax.all_to_all(partial_out, "wr", split_axis=1, concat_axis=0, tiled=True)


def per_device(hidden, weight, expert_ids, gate_score):
    if lax.axis_size("ep") == 16 and lax.axis_size("wr") == 2:
        return by_kernel(hidden, weight, expert_ids, gate_score)
    return by_collectives(hidden, weight, expert_ids, gate_score)


def solution(mesh):
    in_specs = (
        P(("groups", "ep"), None, "wr"),
        P("ep", None, "wr"),
        P(("groups", "ep"), None),
        P(("groups", "ep"), None),
    )
    out_specs = P(("groups", "ep"), "wr")
    return jax.shard_map(
        per_device, mesh=mesh, in_specs=in_specs, out_specs=out_specs, check_vma=False
    )
```

```python
import functools

import jax
import jax.numpy as jnp
from jax import lax
from jax.experimental import pallas as pl
from jax.experimental.pallas import tpu as pltpu
from jax.sharding import PartitionSpec as P

MESH = pl.DeviceIdType.MESH
ORDER = (1, 3, 2, 0)
LAG = 2
EMPTY = 255.0
TILE = 256


def partner(index, step):
    if step == 0:
        return index
    if step == 1:
        return index + 1 - 2 * (index % 2)
    if step == 2:
        return index + 2 - 4 * (index // 2)
    return 3 - index


def iota(shape, axis):
    return lax.broadcasted_iota(jnp.int32, shape, axis)


def onehot(condition):
    return condition.astype(jnp.float32).astype(jnp.bfloat16)


def mm(a, b):
    return jnp.dot(a, b, preferred_element_type=jnp.float32)


def kernel(rows, ids_ref, score_ref, hidden_hbm, weight_hbm, out_ref,
           hidden_ref, weight, outgoing, arrived, result, planar, table, mixer, zsend, zrecv,
           hsem, wsem, d_send, d_recv, f_send, f_recv, p_send, p_recv,
           t_send, t_recv, z_send, z_recv):
    me, w = lax.axis_index("ep"), lax.axis_index("wr")
    zm, pm = me // 4, me % 4
    top, tokens = ids_ref.shape
    pairs, part = hidden_ref.shape
    group = 4 * rows
    width = out_ref.shape[1]

    fetch = pltpu.make_async_copy(hidden_hbm, hidden_ref, hsem)
    fetch.start()
    load = pltpu.make_async_copy(weight_hbm, weight, wsem)
    load.start()

    barrier = pltpu.get_barrier_semaphore()
    for j in range(4):
        for q in range(4):
            if j or q:
                pl.semaphore_signal(
                    barrier, inc=1, device_id_type=MESH,
                    device_id={"ep": partner(zm, j) * 4 + partner(pm, q), "wr": w})
    pl.semaphore_signal(barrier, inc=1, device_id_type=MESH, device_id={"ep": me, "wr": 1 - w})

    ids, score = ids_ref[...], score_ref[...]
    expert_row = iota((16, tokens), 0)
    hits = [ids[k:k + 1] == expert_row for k in range(top)]
    scores = jnp.zeros((16, tokens), jnp.float32)
    for k in range(top):
        scores = scores + jnp.where(hits[k], score[k:k + 1].astype(jnp.float32), 0.0)
    before = mm(onehot(scores > 0), onehot(iota((tokens, tokens), 0) < iota((tokens, tokens), 1)))
    choice = iota((top, tokens), 0)
    slots = jnp.zeros((top, tokens), jnp.float32)
    for k in range(top):
        slot = jnp.sum(jnp.where(hits[k], before, 0.0), axis=0, keepdims=True)
        slots = slots + jnp.where(choice == k, slot, 0.0)

    first = top * iota((tokens, pairs), 0)
    pair = iota((tokens, pairs), 1)
    copies = onehot((pair >= first) & (pair < first + top))
    turn = (lax.rem(iota((top, pairs), 1), top) == iota((top, pairs), 0)).astype(jnp.float32)

    def by_pair(values):
        return jnp.sum(mm(values.astype(jnp.bfloat16), copies) * turn, axis=0, keepdims=True)

    target = (by_pair(ids.astype(jnp.float32)) * rows + by_pair(slots)).astype(jnp.int32)

    def block(ref, j, p):
        return ref.at[j, pl.ds(pl.multiple_of(p * rows, 16), rows)]

    fetch.wait()
    pl.semaphore_wait(barrier, 16)

    dispatch = {}
    for j in ORDER:
        zd = partner(zm, j)
        pick = onehot(target - zd * group == iota((group, pairs), 0))
        outgoing[j] = mm(pick, hidden_ref[...]).astype(jnp.bfloat16)
        for q in range(4):
            pd = partner(pm, q)
            if j == 0 and q == 0:
                arrived[w, 0, pl.ds(pl.multiple_of(pm * rows, 16), rows)] = (
                    outgoing[0, pl.ds(pl.multiple_of(pm * rows, 16), rows)])
                continue
            copy = pltpu.make_async_remote_copy(
                src_ref=block(outgoing, j, pd),
                dst_ref=arrived.at[w, j, pl.ds(pl.multiple_of(pm * rows, 16), rows)],
                send_sem=d_send.at[j, q], recv_sem=d_recv.at[j, q],
                device_id={"ep": zd * 4 + pd, "wr": w}, device_id_type=MESH)
            copy.start()
            dispatch[j, q] = copy

    gates = 2.827 * scores / jnp.sum(scores, axis=0, keepdims=True)
    place = jnp.where(scores > 0, before, EMPTY)
    high = gates.astype(jnp.bfloat16).astype(jnp.float32)
    stacked = jnp.concatenate(
        [place, high, gates - high, jnp.zeros((80, tokens), jnp.float32)], axis=0)
    table[0] = stacked.T.astype(jnp.bfloat16)
    tables = {}
    for j in range(1, 4):
        tables[j] = pltpu.make_async_remote_copy(
            src_ref=table.at[0], dst_ref=table.at[j],
            send_sem=t_send.at[j], recv_sem=t_recv.at[j],
            device_id={"ep": partner(zm, j) * 4 + pm, "wr": w}, device_id_type=MESH)
        tables[j].start()

    planars, forwards, zcopies = {}, {}, {}

    def forward(j):
        for q in range(4):
            if j or q:
                dispatch[j, q].wait_recv()
        forwards[j] = pltpu.make_async_remote_copy(
            src_ref=arrived.at[w, j], dst_ref=arrived.at[w, j],
            send_sem=f_send.at[j], recv_sem=f_recv.at[j],
            device_id={"ep": me, "wr": 1 - w}, device_id_type=MESH)
        forwards[j].start()

    cut = (width // TILE + 1) // 2 * TILE
    chunks = ((0, cut), (cut, width))

    def tiles(c, body):
        low, high = chunks[c]

        @pl.loop(low // TILE, high // TILE)
        def _(i):
            body(pl.ds(pl.multiple_of(i * TILE, TILE), TILE))

    def expert(j, c):
        def body(cols):
            total = mm(arrived[0, j], weight[:part, cols]) + mm(arrived[1, j], weight[part:, cols])
            result[j, :, cols] = total.astype(jnp.bfloat16)

        tiles(c, body)
        chunk = pl.ds(chunks[c][0], chunks[c][1] - chunks[c][0])
        mine = pl.ds(pl.multiple_of(pm * rows, 16), rows)
        for q in (3, 1, 2):
            pd = partner(pm, q)
            theirs = pl.ds(pl.multiple_of(pd * rows, 16), rows)
            planars[j, q, c] = pltpu.make_async_remote_copy(
                src_ref=result.at[j, theirs, chunk], dst_ref=planar.at[j, mine, chunk],
                send_sem=p_send.at[j, q, c], recv_sem=p_recv.at[j, q, c],
                device_id={"ep": zm * 4 + pd, "wr": w}, device_id_type=MESH)
            planars[j, q, c].start()
        planar[j, mine, chunk] = result[j, mine, chunk]

    def spreads(j):
        if j:
            tables[j].wait_recv()
        info = table[j]
        column = iota((128, group), 1)
        quarter = sum((column >= n * rows).astype(jnp.int32) for n in range(1, 4))
        source = zm * 4 + quarter

        def spread(shift):
            return mm(info, onehot(iota((128, group), 0) == source + shift))

        wide = iota((tokens, group), 1)
        within = wide - rows * sum((wide >= n * rows).astype(jnp.int32) for n in range(1, 4))
        hit = spread(0) == within.astype(jnp.float32)
        for part_at in (0, 1):
            values = jnp.where(hit, spread(16 + 16 * part_at), 0.0)
            mixer[j, part_at] = values.astype(jnp.bfloat16)

    def combine(j, c):
        for q in range(1, 4):
            planars[j, q, c].wait_recv()
        if j == 2:
            zcopies[3, c].wait_recv()
        if j == 0:
            zcopies[1, c].wait_recv()
            zcopies[2, c].wait_recv()

        def body(cols):
            values = planar[j, :, cols]
            total = mm(mixer[j, 0], values) + mm(mixer[j, 1], values)
            if j == 2:
                total = total + zrecv[3, :, cols].astype(jnp.float32)
            if j == 0:
                total = (total + zrecv[1, :, cols].astype(jnp.float32)
                         + zrecv[2, :, cols].astype(jnp.float32))
                out_ref[:, cols] = total.astype(jnp.bfloat16)
            else:
                zsend[j, :, cols] = total.astype(jnp.bfloat16)

        tiles(c, body)
        if j:
            chunk = pl.ds(chunks[c][0], chunks[c][1] - chunks[c][0])
            zcopies[j, c] = pltpu.make_async_remote_copy(
                src_ref=zsend.at[j, :, chunk], dst_ref=zrecv.at[j, :, chunk],
                send_sem=z_send.at[j, c], recv_sem=z_recv.at[j, c],
                device_id={"ep": partner(zm, 2 if j == 2 else 1) * 4 + pm, "wr": w},
                device_id_type=MESH)
            zcopies[j, c].start()

    load.wait()
    items = [(j, c) for j in ORDER for c in (0, 1)]
    for n, (j, c) in enumerate(items):
        if c == 0:
            forward(j)
            spreads(j)
            forwards[j].wait_recv()
        expert(j, c)
        if n >= LAG:
            combine(*items[n - LAG])
    for item in items[-LAG:]:
        combine(*item)

    for copies in (dispatch, tables, forwards, planars, zcopies):
        for copy in copies.values():
            copy.wait_send()


def by_kernel(hidden, weight, expert_ids, gate_score):
    tokens, top, part = hidden.shape
    full, width = weight.shape[1:]
    pairs = tokens * top
    rows = 2 * (5 * pairs // 2 // (4 * 16))
    group = 4 * rows
    bf16 = jnp.bfloat16
    vmem = pl.BlockSpec(memory_space=pltpu.VMEM)
    dma = pltpu.SemaphoreType.DMA
    return pl.pallas_call(
        functools.partial(kernel, rows),
        out_shape=jax.ShapeDtypeStruct((tokens, width), bf16),
        in_specs=[vmem, vmem, pl.BlockSpec(memory_space=pl.ANY), pl.BlockSpec(memory_space=pl.ANY)],
        out_specs=vmem,
        scratch_shapes=[
            pltpu.VMEM((pairs, part), bf16),
            pltpu.VMEM((full, width), bf16),
            pltpu.VMEM((4, group, part), bf16),
            pltpu.VMEM((2, 4, group, part), bf16),
            pltpu.VMEM((4, group, width), bf16),
            pltpu.VMEM((4, group, width), bf16),
            pltpu.VMEM((4, tokens, 128), bf16),
            pltpu.VMEM((4, 2, tokens, group), bf16),
            pltpu.VMEM((4, tokens, width), bf16),
            pltpu.VMEM((4, tokens, width), bf16),
            dma, dma, dma((4, 4)), dma((4, 4)), dma((4,)), dma((4,)), dma((4, 4, 2)), dma((4, 4, 2)),
            dma((4,)), dma((4,)), dma((4, 2)), dma((4, 2)),
        ],
        compiler_params=pltpu.CompilerParams(
            collective_id=0, has_side_effects=True, vmem_limit_bytes=50 * 1024 * 1024),
        cost_estimate=pl.CostEstimate(
            flops=2 * 16 * rows * full * width, bytes_accessed=2 * full * width, transcendentals=0),
    )(expert_ids.T, gate_score.T, hidden.reshape(pairs, part), weight[0])


def mixing(gate_score):
    score = gate_score.astype(jnp.float32)
    return 2.827 * score / jnp.sum(score, axis=1, keepdims=True)


def slot_numbers(ids_flat, experts, block_pairs):
    onehot = (ids_flat[:, None] == jnp.arange(experts, dtype=jnp.int32)[None, :]).astype(jnp.int32)
    grouped = onehot.reshape(-1, block_pairs, experts)
    before = jnp.cumsum(grouped, axis=1) - grouped
    return jnp.sum(before * grouped, axis=2).reshape(-1)


def by_collectives(hidden, weight, expert_ids, gate_score):
    tok_dev, top, part_width = hidden.shape
    experts = lax.axis_size("ep")
    half = tok_dev // 2
    cap = max(2, 5 * half * top // (4 * experts))
    side = lax.axis_index("wr")
    gates = mixing(gate_score)
    local_weight = weight[0]
    source = lax.all_gather(hidden, "wr", axis=2, tiled=True)
    start = side * half
    mine = lax.dynamic_slice_in_dim(source, start, half, 0)
    my_ids = lax.dynamic_slice_in_dim(expert_ids, start, half, 0).reshape(-1)
    my_gates = lax.dynamic_slice_in_dim(gates, start, half, 0)
    slot = slot_numbers(my_ids, experts, half * top)
    target = my_ids * cap + slot
    row_width = mine.shape[2]
    outgoing = (
        jnp.zeros((experts * cap, row_width), jnp.bfloat16)
        .at[target]
        .set(mine.reshape(half * top, row_width))
    )
    outgoing = outgoing.reshape(experts, cap, row_width)
    received = lax.all_to_all(outgoing, "ep", split_axis=0, concat_axis=0, tiled=True)
    result = jnp.einsum(
        "scj,jd->scd",
        received,
        lax.all_gather(local_weight, "wr", axis=1, tiled=True),
        preferred_element_type=jnp.float32,
    ).astype(jnp.bfloat16)
    returned = lax.all_to_all(result, "ep", split_axis=0, concat_axis=0, tiled=True)
    full_width = returned.shape[2]
    picked = returned.reshape(experts * cap, full_width)[target]
    weighted = picked.astype(jnp.float32).reshape(half, top, full_width) * my_gates[:, :, None]
    partial_out = jnp.sum(weighted, axis=1).astype(jnp.bfloat16)
    return lax.all_to_all(partial_out, "wr", split_axis=1, concat_axis=0, tiled=True)


def per_device(hidden, weight, expert_ids, gate_score):
    if lax.axis_size("ep") == 16 and lax.axis_size("wr") == 2:
        return by_kernel(hidden, weight, expert_ids, gate_score)
    return by_collectives(hidden, weight, expert_ids, gate_score)


def solution(mesh):
    in_specs = (
        P(("groups", "ep"), None, "wr"),
        P("ep", None, "wr"),
        P(("groups", "ep"), None),
        P(("groups", "ep"), None),
    )
    out_specs = P(("groups", "ep"), "wr")
    return jax.shard_map(
        per_device, mesh=mesh, in_specs=in_specs, out_specs=out_specs, check_vma=False
    )
```

```python
import functools

import jax
import jax.numpy as jnp
from jax import lax
from jax.experimental import pallas as pl
from jax.experimental.pallas import tpu as pltpu
from jax.sharding import PartitionSpec as P

MESH = pl.DeviceIdType.MESH
ORDER = (1, 3, 2, 0)
LAG = 3
PARTS = 3
EMPTY = 255.0
TILE = 256


def partner(index, step):
    if step == 0:
        return index
    if step == 1:
        return index + 1 - 2 * (index % 2)
    if step == 2:
        return index + 2 - 4 * (index // 2)
    return 3 - index


def iota(shape, axis):
    return lax.broadcasted_iota(jnp.int32, shape, axis)


def onehot(condition):
    return condition.astype(jnp.float32).astype(jnp.bfloat16)


def mm(a, b):
    return jnp.dot(a, b, preferred_element_type=jnp.float32)


def kernel(rows, ids_ref, score_ref, hidden_hbm, weight_hbm, out_ref,
           hidden_ref, weight, outgoing, arrived, result, planar, table, mixer, zsend, zrecv,
           hsem, wsem, d_send, d_recv, f_send, f_recv, p_send, p_recv,
           t_send, t_recv, z_send, z_recv):
    me, w = lax.axis_index("ep"), lax.axis_index("wr")
    zm, pm = me // 4, me % 4
    top, tokens = ids_ref.shape
    pairs, part = hidden_ref.shape
    group = 4 * rows
    width = out_ref.shape[1]

    fetch = pltpu.make_async_copy(hidden_hbm, hidden_ref, hsem)
    fetch.start()
    load = pltpu.make_async_copy(weight_hbm, weight, wsem)
    load.start()

    barrier = pltpu.get_barrier_semaphore()
    for j in range(4):
        for q in range(4):
            if j or q:
                pl.semaphore_signal(
                    barrier, inc=1, device_id_type=MESH,
                    device_id={"ep": partner(zm, j) * 4 + partner(pm, q), "wr": w})
    pl.semaphore_signal(barrier, inc=1, device_id_type=MESH, device_id={"ep": me, "wr": 1 - w})

    ids, score = ids_ref[...], score_ref[...]
    expert_row = iota((16, tokens), 0)
    hits = [ids[k:k + 1] == expert_row for k in range(top)]
    scores = jnp.zeros((16, tokens), jnp.float32)
    for k in range(top):
        scores = scores + jnp.where(hits[k], score[k:k + 1].astype(jnp.float32), 0.0)
    before = mm(onehot(scores > 0), onehot(iota((tokens, tokens), 0) < iota((tokens, tokens), 1)))
    choice = iota((top, tokens), 0)
    slots = jnp.zeros((top, tokens), jnp.float32)
    for k in range(top):
        slot = jnp.sum(jnp.where(hits[k], before, 0.0), axis=0, keepdims=True)
        slots = slots + jnp.where(choice == k, slot, 0.0)

    first = top * iota((tokens, pairs), 0)
    pair = iota((tokens, pairs), 1)
    copies = onehot((pair >= first) & (pair < first + top))
    turn = (lax.rem(iota((top, pairs), 1), top) == iota((top, pairs), 0)).astype(jnp.float32)

    def by_pair(values):
        return jnp.sum(mm(values.astype(jnp.bfloat16), copies) * turn, axis=0, keepdims=True)

    target = (by_pair(ids.astype(jnp.float32)) * rows + by_pair(slots)).astype(jnp.int32)

    def block(ref, j, p):
        return ref.at[j, pl.ds(pl.multiple_of(p * rows, 16), rows)]

    fetch.wait()
    pl.semaphore_wait(barrier, 16)

    dispatch = {}
    for j in ORDER:
        zd = partner(zm, j)
        pick = onehot(target - zd * group == iota((group, pairs), 0))
        outgoing[j] = mm(pick, hidden_ref[...]).astype(jnp.bfloat16)
        for q in (3, 2, 1, 0):
            pd = partner(pm, q)
            if j == 0 and q == 0:
                arrived[w, 0, pl.ds(pl.multiple_of(pm * rows, 16), rows)] = (
                    outgoing[0, pl.ds(pl.multiple_of(pm * rows, 16), rows)])
                continue
            copy = pltpu.make_async_remote_copy(
                src_ref=block(outgoing, j, pd),
                dst_ref=arrived.at[w, j, pl.ds(pl.multiple_of(pm * rows, 16), rows)],
                send_sem=d_send.at[j, q], recv_sem=d_recv.at[j, q],
                device_id={"ep": zd * 4 + pd, "wr": w}, device_id_type=MESH)
            copy.start()
            dispatch[j, q] = copy

    gates = 2.827 * scores / jnp.sum(scores, axis=0, keepdims=True)
    place = jnp.where(scores > 0, before, EMPTY)
    high = gates.astype(jnp.bfloat16).astype(jnp.float32)
    stacked = jnp.concatenate(
        [place, high, gates - high, jnp.zeros((80, tokens), jnp.float32)], axis=0)
    table[0] = stacked.T.astype(jnp.bfloat16)
    tables = {}
    for j in range(1, 4):
        tables[j] = pltpu.make_async_remote_copy(
            src_ref=table.at[0], dst_ref=table.at[j],
            send_sem=t_send.at[j], recv_sem=t_recv.at[j],
            device_id={"ep": partner(zm, j) * 4 + pm, "wr": w}, device_id_type=MESH)
        tables[j].start()

    planars, forwards, zcopies = {}, {}, {}

    def forward(j):
        for q in range(4):
            if j or q:
                dispatch[j, q].wait_recv()
        forwards[j] = pltpu.make_async_remote_copy(
            src_ref=arrived.at[w, j], dst_ref=arrived.at[w, j],
            send_sem=f_send.at[j], recv_sem=f_recv.at[j],
            device_id={"ep": me, "wr": 1 - w}, device_id_type=MESH)
        forwards[j].start()

    cuts = [width // TILE * n // PARTS * TILE for n in range(PARTS + 1)]
    chunks = list(zip(cuts[:-1], cuts[1:]))

    def tiles(c, body):
        low, high = chunks[c]

        @pl.loop(low // TILE, high // TILE)
        def _(i):
            body(pl.ds(pl.multiple_of(i * TILE, TILE), TILE))

    def expert(j, c):
        def body(cols):
            total = mm(arrived[0, j], weight[:part, cols]) + mm(arrived[1, j], weight[part:, cols])
            result[j, :, cols] = total.astype(jnp.bfloat16)

        tiles(c, body)
        chunk = pl.ds(chunks[c][0], chunks[c][1] - chunks[c][0])
        mine = pl.ds(pl.multiple_of(pm * rows, 16), rows)
        for q in (1, 2, 3):
            pd = partner(pm, q)
            theirs = pl.ds(pl.multiple_of(pd * rows, 16), rows)
            planars[j, q, c] = pltpu.make_async_remote_copy(
                src_ref=result.at[j, theirs, chunk], dst_ref=planar.at[j, mine, chunk],
                send_sem=p_send.at[j, q, c], recv_sem=p_recv.at[j, q, c],
                device_id={"ep": zm * 4 + pd, "wr": w}, device_id_type=MESH)
            planars[j, q, c].start()
        planar[j, mine, chunk] = result[j, mine, chunk]

    def spreads(j):
        if j:
            tables[j].wait_recv()
        info = table[j]
        column = iota((128, group), 1)
        quarter = sum((column >= n * rows).astype(jnp.int32) for n in range(1, 4))
        source = zm * 4 + quarter

        def spread(shift):
            return mm(info, onehot(iota((128, group), 0) == source + shift))

        wide = iota((tokens, group), 1)
        within = wide - rows * sum((wide >= n * rows).astype(jnp.int32) for n in range(1, 4))
        hit = spread(0) == within.astype(jnp.float32)
        for part_at in (0, 1):
            values = jnp.where(hit, spread(16 + 16 * part_at), 0.0)
            mixer[j, part_at] = values.astype(jnp.bfloat16)

    def combine(j, c):
        for q in range(1, 4):
            planars[j, q, c].wait_recv()
        if j == 2:
            zcopies[3, c].wait_recv()
        if j == 0:
            zcopies[1, c].wait_recv()
            zcopies[2, c].wait_recv()

        def body(cols):
            values = planar[j, :, cols]
            total = mm(mixer[j, 0], values) + mm(mixer[j, 1], values)
            if j == 2:
                total = total + zrecv[3, :, cols].astype(jnp.float32)
            if j == 0:
                total = (total + zrecv[1, :, cols].astype(jnp.float32)
                         + zrecv[2, :, cols].astype(jnp.float32))
                out_ref[:, cols] = total.astype(jnp.bfloat16)
            else:
                zsend[j, :, cols] = total.astype(jnp.bfloat16)

        tiles(c, body)
        if j:
            chunk = pl.ds(chunks[c][0], chunks[c][1] - chunks[c][0])
            zcopies[j, c] = pltpu.make_async_remote_copy(
                src_ref=zsend.at[j, :, chunk], dst_ref=zrecv.at[j, :, chunk],
                send_sem=z_send.at[j, c], recv_sem=z_recv.at[j, c],
                device_id={"ep": partner(zm, 2 if j == 2 else 1) * 4 + pm, "wr": w},
                device_id_type=MESH)
            zcopies[j, c].start()

    load.wait()
    items = [(j, c) for j in ORDER for c in range(PARTS)]
    for n, (j, c) in enumerate(items):
        if c == 0:
            forward(j)
            spreads(j)
            forwards[j].wait_recv()
        expert(j, c)
        if n >= LAG:
            combine(*items[n - LAG])
    for item in items[-LAG:]:
        combine(*item)

    for copies in (dispatch, tables, forwards, planars, zcopies):
        for copy in copies.values():
            copy.wait_send()


def by_kernel(hidden, weight, expert_ids, gate_score):
    tokens, top, part = hidden.shape
    full, width = weight.shape[1:]
    pairs = tokens * top
    rows = 2 * (5 * pairs // 2 // (4 * 16))
    group = 4 * rows
    bf16 = jnp.bfloat16
    vmem = pl.BlockSpec(memory_space=pltpu.VMEM)
    dma = pltpu.SemaphoreType.DMA
    return pl.pallas_call(
        functools.partial(kernel, rows),
        out_shape=jax.ShapeDtypeStruct((tokens, width), bf16),
        in_specs=[vmem, vmem, pl.BlockSpec(memory_space=pl.ANY), pl.BlockSpec(memory_space=pl.ANY)],
        out_specs=vmem,
        scratch_shapes=[
            pltpu.VMEM((pairs, part), bf16),
            pltpu.VMEM((full, width), bf16),
            pltpu.VMEM((4, group, part), bf16),
            pltpu.VMEM((2, 4, group, part), bf16),
            pltpu.VMEM((4, group, width), bf16),
            pltpu.VMEM((4, group, width), bf16),
            pltpu.VMEM((4, tokens, 128), bf16),
            pltpu.VMEM((4, 2, tokens, group), bf16),
            pltpu.VMEM((4, tokens, width), bf16),
            pltpu.VMEM((4, tokens, width), bf16),
            dma, dma, dma((4, 4)), dma((4, 4)), dma((4,)), dma((4,)), dma((4, 4, PARTS)), dma((4, 4, PARTS)),
            dma((4,)), dma((4,)), dma((4, PARTS)), dma((4, PARTS)),
        ],
        compiler_params=pltpu.CompilerParams(
            collective_id=0, has_side_effects=True, vmem_limit_bytes=50 * 1024 * 1024),
        cost_estimate=pl.CostEstimate(
            flops=2 * 16 * rows * full * width, bytes_accessed=2 * full * width, transcendentals=0),
    )(expert_ids.T, gate_score.T, hidden.reshape(pairs, part), weight[0])


def mixing(gate_score):
    score = gate_score.astype(jnp.float32)
    return 2.827 * score / jnp.sum(score, axis=1, keepdims=True)


def slot_numbers(ids_flat, experts, block_pairs):
    onehot = (ids_flat[:, None] == jnp.arange(experts, dtype=jnp.int32)[None, :]).astype(jnp.int32)
    grouped = onehot.reshape(-1, block_pairs, experts)
    before = jnp.cumsum(grouped, axis=1) - grouped
    return jnp.sum(before * grouped, axis=2).reshape(-1)


def by_collectives(hidden, weight, expert_ids, gate_score):
    tok_dev, top, part_width = hidden.shape
    experts = lax.axis_size("ep")
    half = tok_dev // 2
    cap = max(2, 5 * half * top // (4 * experts))
    side = lax.axis_index("wr")
    gates = mixing(gate_score)
    local_weight = weight[0]
    source = lax.all_gather(hidden, "wr", axis=2, tiled=True)
    start = side * half
    mine = lax.dynamic_slice_in_dim(source, start, half, 0)
    my_ids = lax.dynamic_slice_in_dim(expert_ids, start, half, 0).reshape(-1)
    my_gates = lax.dynamic_slice_in_dim(gates, start, half, 0)
    slot = slot_numbers(my_ids, experts, half * top)
    target = my_ids * cap + slot
    row_width = mine.shape[2]
    outgoing = (
        jnp.zeros((experts * cap, row_width), jnp.bfloat16)
        .at[target]
        .set(mine.reshape(half * top, row_width))
    )
    outgoing = outgoing.reshape(experts, cap, row_width)
    received = lax.all_to_all(outgoing, "ep", split_axis=0, concat_axis=0, tiled=True)
    result = jnp.einsum(
        "scj,jd->scd",
        received,
        lax.all_gather(local_weight, "wr", axis=1, tiled=True),
        preferred_element_type=jnp.float32,
    ).astype(jnp.bfloat16)
    returned = lax.all_to_all(result, "ep", split_axis=0, concat_axis=0, tiled=True)
    full_width = returned.shape[2]
    picked = returned.reshape(experts * cap, full_width)[target]
    weighted = picked.astype(jnp.float32).reshape(half, top, full_width) * my_gates[:, :, None]
    partial_out = jnp.sum(weighted, axis=1).astype(jnp.bfloat16)
    return lax.all_to_all(partial_out, "wr", split_axis=1, concat_axis=0, tiled=True)


def per_device(hidden, weight, expert_ids, gate_score):
    if lax.axis_size("ep") == 16 and lax.axis_size("wr") == 2:
        return by_kernel(hidden, weight, expert_ids, gate_score)
    return by_collectives(hidden, weight, expert_ids, gate_score)


def solution(mesh):
    in_specs = (
        P(("groups", "ep"), None, "wr"),
        P("ep", None, "wr"),
        P(("groups", "ep"), None),
        P(("groups", "ep"), None),
    )
    out_specs = P(("groups", "ep"), "wr")
    return jax.shard_map(
        per_device, mesh=mesh, in_specs=in_specs, out_specs=out_specs, check_vma=False
    )
```

```python
import functools

import jax
import jax.numpy as jnp
from jax import lax
from jax.experimental import pallas as pl
from jax.experimental.pallas import tpu as pltpu
from jax.sharding import PartitionSpec as P

MESH = pl.DeviceIdType.MESH
ORDER = (1, 3, 2, 0)
LAG = 3
PARTS = 3
EMPTY = 255.0
TILE = 256


def partner(index, step):
    if step == 0:
        return index
    if step == 1:
        return index + 1 - 2 * (index % 2)
    if step == 2:
        return index + 2 - 4 * (index // 2)
    return 3 - index


def iota(shape, axis):
    return lax.broadcasted_iota(jnp.int32, shape, axis)


def onehot(condition):
    return condition.astype(jnp.float32).astype(jnp.bfloat16)


def mm(a, b):
    return jnp.dot(a, b, preferred_element_type=jnp.float32)


def kernel(rows, ids_ref, score_ref, hidden_hbm, weight_hbm, out_ref,
           hidden_ref, weight, outgoing, arrived, result, planar, table, mixer, zsend, zrecv,
           hsem, wsem, d_send, d_recv, f_send, f_recv, p_send, p_recv,
           t_send, t_recv, z_send, z_recv):
    me, w = lax.axis_index("ep"), lax.axis_index("wr")
    zm, pm = me // 4, me % 4
    top, tokens = ids_ref.shape
    pairs, part = hidden_ref.shape
    group = 4 * rows
    width = out_ref.shape[1]

    fetch = pltpu.make_async_copy(hidden_hbm, hidden_ref, hsem)
    fetch.start()
    load = pltpu.make_async_copy(weight_hbm, weight, wsem)
    load.start()

    barrier = pltpu.get_barrier_semaphore()
    for j in range(4):
        for q in range(4):
            if j or q:
                pl.semaphore_signal(
                    barrier, inc=1, device_id_type=MESH,
                    device_id={"ep": partner(zm, j) * 4 + partner(pm, q), "wr": w})
    pl.semaphore_signal(barrier, inc=1, device_id_type=MESH, device_id={"ep": me, "wr": 1 - w})

    ids, score = ids_ref[...], score_ref[...]
    expert_row = iota((16, tokens), 0)
    hits = [ids[k:k + 1] == expert_row for k in range(top)]
    scores = jnp.zeros((16, tokens), jnp.float32)
    for k in range(top):
        scores = scores + jnp.where(hits[k], score[k:k + 1].astype(jnp.float32), 0.0)
    before = mm(onehot(scores > 0), onehot(iota((tokens, tokens), 0) < iota((tokens, tokens), 1)))
    choice = iota((top, tokens), 0)
    slots = jnp.zeros((top, tokens), jnp.float32)
    for k in range(top):
        slot = jnp.sum(jnp.where(hits[k], before, 0.0), axis=0, keepdims=True)
        slots = slots + jnp.where(choice == k, slot, 0.0)

    first = top * iota((tokens, pairs), 0)
    pair = iota((tokens, pairs), 1)
    copies = onehot((pair >= first) & (pair < first + top))
    turn = (lax.rem(iota((top, pairs), 1), top) == iota((top, pairs), 0)).astype(jnp.float32)

    def by_pair(values):
        return jnp.sum(mm(values.astype(jnp.bfloat16), copies) * turn, axis=0, keepdims=True)

    target = (by_pair(ids.astype(jnp.float32)) * rows + by_pair(slots)).astype(jnp.int32)

    def block(ref, j, p):
        return ref.at[j, pl.ds(pl.multiple_of(p * rows, 16), rows)]

    fetch.wait()
    pl.semaphore_wait(barrier, 16)

    dispatch = {}
    for j in ORDER:
        zd = partner(zm, j)
        pick = onehot(target - zd * group == iota((group, pairs), 0))
        outgoing[j] = mm(pick, hidden_ref[...]).astype(jnp.bfloat16)
        for q in (3, 2, 1, 0):
            pd = partner(pm, q)
            if j == 0 and q == 0:
                arrived[w, 0, pl.ds(pl.multiple_of(pm * rows, 16), rows)] = (
                    outgoing[0, pl.ds(pl.multiple_of(pm * rows, 16), rows)])
                continue
            copy = pltpu.make_async_remote_copy(
                src_ref=block(outgoing, j, pd),
                dst_ref=arrived.at[w, j, pl.ds(pl.multiple_of(pm * rows, 16), rows)],
                send_sem=d_send.at[j, q], recv_sem=d_recv.at[j, q],
                device_id={"ep": zd * 4 + pd, "wr": w}, device_id_type=MESH)
            copy.start()
            dispatch[j, q] = copy

    gates = 2.827 * scores / jnp.sum(scores, axis=0, keepdims=True)
    place = jnp.where(scores > 0, before, EMPTY)
    high = gates.astype(jnp.bfloat16).astype(jnp.float32)
    stacked = jnp.concatenate(
        [place, high, gates - high, jnp.zeros((80, tokens), jnp.float32)], axis=0)
    table[0] = stacked.T.astype(jnp.bfloat16)
    tables = {}
    for j in range(1, 4):
        tables[j] = pltpu.make_async_remote_copy(
            src_ref=table.at[0], dst_ref=table.at[j],
            send_sem=t_send.at[j], recv_sem=t_recv.at[j],
            device_id={"ep": partner(zm, j) * 4 + pm, "wr": w}, device_id_type=MESH)
        tables[j].start()

    planars, forwards, zcopies = {}, {}, {}

    def forward(j):
        for q in range(4):
            if j or q:
                dispatch[j, q].wait_recv()
        forwards[j] = pltpu.make_async_remote_copy(
            src_ref=arrived.at[w, j], dst_ref=arrived.at[w, j],
            send_sem=f_send.at[j], recv_sem=f_recv.at[j],
            device_id={"ep": me, "wr": 1 - w}, device_id_type=MESH)
        forwards[j].start()

    cuts = [width // TILE * n // PARTS * TILE for n in range(PARTS + 1)]
    chunks = list(zip(cuts[:-1], cuts[1:]))

    def tiles(c, body):
        low, high = chunks[c]

        @pl.loop(low // TILE, high // TILE)
        def _(i):
            body(pl.ds(pl.multiple_of(i * TILE, TILE), TILE))

    def expert(j, c):
        def body(cols):
            total = mm(arrived[0, j], weight[:part, cols]) + mm(arrived[1, j], weight[part:, cols])
            result[j, :, cols] = total.astype(jnp.bfloat16)

        tiles(c, body)
        chunk = pl.ds(chunks[c][0], chunks[c][1] - chunks[c][0])
        mine = pl.ds(pl.multiple_of(pm * rows, 16), rows)
        for q in (1, 2, 3):
            pd = partner(pm, q)
            theirs = pl.ds(pl.multiple_of(pd * rows, 16), rows)
            planars[j, q, c] = pltpu.make_async_remote_copy(
                src_ref=result.at[j, theirs, chunk], dst_ref=planar.at[j, mine, chunk],
                send_sem=p_send.at[j, q, c], recv_sem=p_recv.at[j, q, c],
                device_id={"ep": zm * 4 + pd, "wr": w}, device_id_type=MESH)
            planars[j, q, c].start()
        planar[j, mine, chunk] = result[j, mine, chunk]

    def spreads(j):
        if j:
            tables[j].wait_recv()
        info = table[j]
        column = iota((128, group), 1)
        quarter = sum((column >= n * rows).astype(jnp.int32) for n in range(1, 4))
        source = zm * 4 + quarter

        def spread(shift):
            return mm(info, onehot(iota((128, group), 0) == source + shift))

        wide = iota((tokens, group), 1)
        within = wide - rows * sum((wide >= n * rows).astype(jnp.int32) for n in range(1, 4))
        hit = spread(0) == within.astype(jnp.float32)
        for part_at in (0, 1):
            values = jnp.where(hit, spread(16 + 16 * part_at), 0.0)
            mixer[j, part_at] = values.astype(jnp.bfloat16)

    def combine(j, c):
        for q in range(1, 4):
            planars[j, q, c].wait_recv()
        if j == 2:
            zcopies[3, c].wait_recv()
        if j == 0:
            zcopies[1, c].wait_recv()
            zcopies[2, c].wait_recv()

        def body(cols):
            values = planar[j, :, cols]
            total = mm(mixer[j, 0], values) + mm(mixer[j, 1], values)
            if j == 2:
                total = total + zrecv[3, :, cols].astype(jnp.float32)
            if j == 0:
                total = (total + zrecv[1, :, cols].astype(jnp.float32)
                         + zrecv[2, :, cols].astype(jnp.float32))
                out_ref[:, cols] = total.astype(jnp.bfloat16)
            else:
                zsend[j, :, cols] = total.astype(jnp.bfloat16)

        tiles(c, body)
        if j:
            chunk = pl.ds(chunks[c][0], chunks[c][1] - chunks[c][0])
            zcopies[j, c] = pltpu.make_async_remote_copy(
                src_ref=zsend.at[j, :, chunk], dst_ref=zrecv.at[j, :, chunk],
                send_sem=z_send.at[j, c], recv_sem=z_recv.at[j, c],
                device_id={"ep": partner(zm, 2 if j == 2 else 1) * 4 + pm, "wr": w},
                device_id_type=MESH)
            zcopies[j, c].start()

    load.wait()
    items = [(j, c) for j in ORDER for c in range(PARTS)]
    for n, (j, c) in enumerate(items):
        if c == 0:
            if j == 2:
                forward(0)
            if j:
                forward(j)
            spreads(j)
            forwards[j].wait_recv()
        expert(j, c)
        if n >= LAG:
            combine(*items[n - LAG])
    for item in items[-LAG:]:
        combine(*item)

    for copies in (dispatch, tables, forwards, planars, zcopies):
        for copy in copies.values():
            copy.wait_send()


def by_kernel(hidden, weight, expert_ids, gate_score):
    tokens, top, part = hidden.shape
    full, width = weight.shape[1:]
    pairs = tokens * top
    rows = 2 * (5 * pairs // 2 // (4 * 16))
    group = 4 * rows
    bf16 = jnp.bfloat16
    vmem = pl.BlockSpec(memory_space=pltpu.VMEM)
    dma = pltpu.SemaphoreType.DMA
    return pl.pallas_call(
        functools.partial(kernel, rows),
        out_shape=jax.ShapeDtypeStruct((tokens, width), bf16),
        in_specs=[vmem, vmem, pl.BlockSpec(memory_space=pl.ANY), pl.BlockSpec(memory_space=pl.ANY)],
        out_specs=vmem,
        scratch_shapes=[
            pltpu.VMEM((pairs, part), bf16),
            pltpu.VMEM((full, width), bf16),
            pltpu.VMEM((4, group, part), bf16),
            pltpu.VMEM((2, 4, group, part), bf16),
            pltpu.VMEM((4, group, width), bf16),
            pltpu.VMEM((4, group, width), bf16),
            pltpu.VMEM((4, tokens, 128), bf16),
            pltpu.VMEM((4, 2, tokens, group), bf16),
            pltpu.VMEM((4, tokens, width), bf16),
            pltpu.VMEM((4, tokens, width), bf16),
            dma, dma, dma((4, 4)), dma((4, 4)), dma((4,)), dma((4,)), dma((4, 4, PARTS)), dma((4, 4, PARTS)),
            dma((4,)), dma((4,)), dma((4, PARTS)), dma((4, PARTS)),
        ],
        compiler_params=pltpu.CompilerParams(
            collective_id=0, has_side_effects=True, vmem_limit_bytes=50 * 1024 * 1024),
        cost_estimate=pl.CostEstimate(
            flops=2 * 16 * rows * full * width, bytes_accessed=2 * full * width, transcendentals=0),
    )(expert_ids.T, gate_score.T, hidden.reshape(pairs, part), weight[0])


def mixing(gate_score):
    score = gate_score.astype(jnp.float32)
    return 2.827 * score / jnp.sum(score, axis=1, keepdims=True)


def slot_numbers(ids_flat, experts, block_pairs):
    onehot = (ids_flat[:, None] == jnp.arange(experts, dtype=jnp.int32)[None, :]).astype(jnp.int32)
    grouped = onehot.reshape(-1, block_pairs, experts)
    before = jnp.cumsum(grouped, axis=1) - grouped
    return jnp.sum(before * grouped, axis=2).reshape(-1)


def by_collectives(hidden, weight, expert_ids, gate_score):
    tok_dev, top, part_width = hidden.shape
    experts = lax.axis_size("ep")
    half = tok_dev // 2
    cap = max(2, 5 * half * top // (4 * experts))
    side = lax.axis_index("wr")
    gates = mixing(gate_score)
    local_weight = weight[0]
    source = lax.all_gather(hidden, "wr", axis=2, tiled=True)
    start = side * half
    mine = lax.dynamic_slice_in_dim(source, start, half, 0)
    my_ids = lax.dynamic_slice_in_dim(expert_ids, start, half, 0).reshape(-1)
    my_gates = lax.dynamic_slice_in_dim(gates, start, half, 0)
    slot = slot_numbers(my_ids, experts, half * top)
    target = my_ids * cap + slot
    row_width = mine.shape[2]
    outgoing = (
        jnp.zeros((experts * cap, row_width), jnp.bfloat16)
        .at[target]
        .set(mine.reshape(half * top, row_width))
    )
    outgoing = outgoing.reshape(experts, cap, row_width)
    received = lax.all_to_all(outgoing, "ep", split_axis=0, concat_axis=0, tiled=True)
    result = jnp.einsum(
        "scj,jd->scd",
        received,
        lax.all_gather(local_weight, "wr", axis=1, tiled=True),
        preferred_element_type=jnp.float32,
    ).astype(jnp.bfloat16)
    returned = lax.all_to_all(result, "ep", split_axis=0, concat_axis=0, tiled=True)
    full_width = returned.shape[2]
    picked = returned.reshape(experts * cap, full_width)[target]
    weighted = picked.astype(jnp.float32).reshape(half, top, full_width) * my_gates[:, :, None]
    partial_out = jnp.sum(weighted, axis=1).astype(jnp.bfloat16)
    return lax.all_to_all(partial_out, "wr", split_axis=1, concat_axis=0, tiled=True)


def per_device(hidden, weight, expert_ids, gate_score):
    if lax.axis_size("ep") == 16 and lax.axis_size("wr") == 2:
        return by_kernel(hidden, weight, expert_ids, gate_score)
    return by_collectives(hidden, weight, expert_ids, gate_score)


def solution(mesh):
    in_specs = (
        P(("groups", "ep"), None, "wr"),
        P("ep", None, "wr"),
        P(("groups", "ep"), None),
        P(("groups", "ep"), None),
    )
    out_specs = P(("groups", "ep"), "wr")
    return jax.shard_map(
        per_device, mesh=mesh, in_specs=in_specs, out_specs=out_specs, check_vma=False
    )
```
